32 devices in a mesh: row: 8 (over z, x), col: 4 (over y, core).
Axes of the slice: x: 2, y: 2, z: 4, core: 2. Of those that a mesh axis runs over, the one named last changes fastest.
Arguments:
- tokens: bfloat16 [80, 8192], P('row', 'col'), may hold values from -6 to 6
- w_gate: bfloat16 [8192, 16384], P('row', 'col'), may hold values from -0.0625 to 0.0625
- w_up: bfloat16 [8192, 16384], P('row', 'col'), may hold values from -0.0625 to 0.0625
- w_down: bfloat16 [16384, 8192], P('row', 'col'), may hold values from -0.046875 to 0.046875
- out_grad: bfloat16 [80, 8192], P('row', 'col'), may hold values from -4 to 4
Outputs:
- output: bfloat16 [80, 8192], P('row', 'col')
- grad_tokens: bfloat16 [80, 8192], P('row', 'col')
- grad_gate: bfloat16 [8192, 16384], P('row', 'col')
- grad_up: bfloat16 [8192, 16384], P('row', 'col')
- grad_down: bfloat16 [16384, 8192], P('row', 'col')
The draws below stay inside these ranges and needn't reach their ends.
All inputs are finite; a program needn't handle non-finite values.
Results may differ from the reference program's by a relative error of at most 0.0051.
Values may be sent and summed in bfloat16 or wider, within the bound.
A program may use at most 128 MiB of HBM per device.

```python
import jax
import jax.numpy as jnp

D = 8192
FF = 16384
TOKENS = 80


def level_of(stream_key, shape, pieces, low, top_value):
    loudness, own = 1.0, jax.random.fold_in(stream_key, 6)
    for dim, shards_of in pieces:
        heights = jnp.exp(jax.random.uniform(jax.random.fold_in(own, dim), (shards_of,), jnp.float32, low / len(pieces), top_value / len(pieces)))
        loudness = loudness * jnp.repeat(heights, shape[dim] // shards_of).reshape([-1 if axis == dim else 1 for axis in range(len(shape))])
    return loudness


def noise(rng, extent, width, reach, cuts=(), dtype=jnp.bfloat16):
    values = jax.random.normal(rng, extent, jnp.float32) * width
    if len(cuts) > 0:
        values = level_of(rng, extent, cuts, -0.22, 0.18) * values
    return jnp.clip(values, min=-reach, max=reach).astype(dtype)


def setup_inputs(seed: int = 0) -> dict:
    splits = jax.random.split(jax.random.key(seed), 6)
    return {
        "tokens": noise(splits[0], (TOKENS, D), 1.0, 6.0, ((0, 8), (1, 4))),
        "w_gate": noise(splits[1], (D, FF), D ** -0.5, 0.0625, ((0, 8), (1, 4))),
        "w_up": noise(splits[2], (D, FF), D ** -0.5, 0.0625, ((0, 8), (1, 4))),
        "w_down": noise(splits[3], (FF, D), FF ** -0.5, 0.046875, ((0, 8), (1, 4))),
        "out_grad": noise(splits[4], (TOKENS, D), 0.3, 4.0, ((0, 8), (1, 4))),
    }


def reference(tokens, w_gate, w_up, w_down, out_grad):
    gate = jnp.dot(tokens, w_gate, preferred_element_type=jnp.float32)
    up = jnp.dot(tokens, w_up, preferred_element_type=jnp.float32)
    sigmoid_gate = jax.nn.sigmoid(gate)
    activated = gate * sigmoid_gate
    hidden = (activated * up).astype(jnp.bfloat16)
    output = jnp.dot(hidden, w_down, preferred_element_type=jnp.float32).astype(jnp.bfloat16)
    grad_hidden = jnp.dot(out_grad, w_down.T, preferred_element_type=jnp.float32)
    grad_act_gate = (grad_hidden * up * sigmoid_gate * (1.0 + gate * (1.0 - sigmoid_gate))).astype(jnp.bfloat16)
    grad_act_up = (grad_hidden * activated).astype(jnp.bfloat16)
    grad_down = jnp.dot(hidden.T, out_grad, preferred_element_type=jnp.float32).astype(jnp.bfloat16)
    grad_gate = jnp.dot(tokens.T, grad_act_gate, preferred_element_type=jnp.float32).astype(jnp.bfloat16)
    grad_up = jnp.dot(tokens.T, grad_act_up, preferred_element_type=jnp.float32).astype(jnp.bfloat16)
    grad_tokens = (jnp.dot(grad_act_gate, w_gate.T, preferred_element_type=jnp.float32)
                   + jnp.dot(grad_act_up, w_up.T, preferred_element_type=jnp.float32)).astype(jnp.bfloat16)
    return output, grad_tokens, grad_gate, grad_up, grad_down
```

```python
import functools

import jax
import jax.numpy as jnp
import numpy as np
from jax import lax
from jax.experimental import pallas as pl
from jax.experimental.pallas import tpu as pltpu
from jax.sharding import PartitionSpec as P

rows_contract = (((0,), (0,)), ((), ()))
cols_contract = (((1,), (1,)), ((), ()))


def broadcast(x, axis, root):
    mine = lax.axis_index(axis) == root
    return lax.psum(jnp.where(mine, x, jnp.zeros_like(x)), axis)


def per_device(tokens, w_gate, w_up, w_down, out_grad):
    row_index = lax.axis_index("row")
    col_index = lax.axis_index("col")
    tok_rows = tokens.shape[0]
    ff_cols = w_gate.shape[1]
    tokens_all, cotangent_all = (
        lax.all_gather(tokens, "row", axis=0, tiled=True),
        lax.all_gather(out_grad, "row", axis=0, tiled=True),
    )

    def to_row_blocks(matrix):
        piece_cols = matrix.shape[1] // 2
        picked = lax.dynamic_slice_in_dim(matrix, row_index % 2 * piece_cols, piece_cols, 1)
        return broadcast(picked, "col", row_index // 2)

    def to_col_blocks(matrix):
        pieces = []
        for offset in range(2):
            pieces.append(broadcast(matrix, "row", 2 * col_index + offset))
        return jnp.concatenate(pieces, axis=1)

    def col_total(matrix):
        return lax.psum(matrix, "col")

    tokens_rows = to_row_blocks(tokens_all)
    block = tokens_rows
    gate_up = lax.psum_scatter(
        jnp.concatenate(
            [
                jnp.dot(block, w_gate, preferred_element_type=jnp.float32),
                jnp.dot(block, w_up, preferred_element_type=jnp.float32),
            ],
            axis=1,
        ),
        "row",
        scatter_dimension=0,
        tiled=True,
    )
    gate = gate_up[:, :ff_cols]
    up = gate_up[:, ff_cols:]
    sigmoid_gate = jax.nn.sigmoid(gate)
    activated = gate * sigmoid_gate
    hidden_share = (activated * up).astype(jnp.bfloat16)
    hidden_all = lax.all_gather(hidden_share, "row", axis=0, tiled=True)
    hidden_rows = to_row_blocks(hidden_all)
    block = hidden_rows
    output = lax.psum_scatter(
        jnp.dot(block, w_down, preferred_element_type=jnp.float32),
        "row",
        scatter_dimension=0,
        tiled=True,
    ).astype(jnp.bfloat16)
    grad_down = lax.dot_general(
        hidden_rows, cotangent_all, rows_contract, preferred_element_type=jnp.float32
    ).astype(jnp.bfloat16)
    hidden_part = lax.dot_general(
        cotangent_all, w_down, cols_contract, preferred_element_type=jnp.float32
    )
    grad_hidden = to_col_blocks(col_total(hidden_part))
    grad_share = lax.dynamic_slice_in_dim(grad_hidden, row_index * tok_rows, tok_rows, 0)
    gate_term = (grad_share * up * sigmoid_gate * (1.0 + gate * (1.0 - sigmoid_gate))).astype(
        jnp.bfloat16
    )
    up_term = (grad_share * activated).astype(jnp.bfloat16)
    gate_grads, up_grads = (
        lax.all_gather(gate_term, "row", axis=0, tiled=True),
        lax.all_gather(up_term, "row", axis=0, tiled=True),
    )
    grad_gate = lax.dot_general(
        tokens_rows, gate_grads, rows_contract, preferred_element_type=jnp.float32
    ).astype(jnp.bfloat16)
    grad_up = lax.dot_general(
        tokens_rows, up_grads, rows_contract, preferred_element_type=jnp.float32
    ).astype(jnp.bfloat16)
    input_part = lax.dot_general(
        gate_grads, w_gate, cols_contract, preferred_element_type=jnp.float32
    ) + lax.dot_general(up_grads, w_up, cols_contract, preferred_element_type=jnp.float32)
    input_cols = to_col_blocks(col_total(input_part))
    grad_tokens = lax.dynamic_slice_in_dim(input_cols, row_index * tok_rows, tok_rows, 0).astype(
        jnp.bfloat16
    )
    return (output, grad_tokens, grad_gate, grad_up, grad_down)


MESH = pl.DeviceIdType.MESH
PAD = 16
f32, bf16 = jnp.float32, jnp.bfloat16


def mm(a, b):
    return jnp.dot(a, b, preferred_element_type=f32)


def mm_t(a, b):
    return lax.dot_general(a, b, cols_contract, preferred_element_type=f32)


def layer(
    R, C,
    tok, og, wg_hbm, wu_hbm, wd_hbm, ex,
    out, gtok, toks, cot, hid, gg, ug,
    wg, wu, wd, tokbuf, ogbuf, own, xsend, xrecv, zsend, zrecv, gupd,
    ghsend, ghrecv, ghsum, ghfin, hsend, hbuf, tbuf, hex_, po, fxrecv, fzsend, fzrecv,
    acc, grecv, gsum, gtbuf,
    w_sem, tok_s, tok_r, og_s, og_r, x_s, x_r, z_s, z_r, gh_s, gh_r, gh2_s, gh2_r,
    h_s, h_r, t_s, t_r, tf_s, fx_s, fx_r, fz_s, fz_r, g_s, g_r, g2_s, g2_r,
):
    r, c = lax.axis_index("row"), lax.axis_index("col")
    H, Z = R // C, R // 2
    z, x = r // 2, r % 2
    mate = z * 2 + (1 - x)
    S = wg.shape[1] // R
    Dr = wg.shape[0]

    def rc(src, dst, ss, rs, dr, dc):
        return pltpu.make_async_remote_copy(
            src_ref=src, dst_ref=dst, send_sem=ss, recv_sem=rs,
            device_id=(dr, dc), device_id_type=MESH,
        )

    def start_any(src, dst, ss, rs, dr, dc):
        here = jnp.logical_and(dr == r, dc == c)

        @pl.when(jnp.logical_not(here))
        def _():
            rc(src, dst, ss, rs, dr, dc).start()

        @pl.when(here)
        def _():
            pltpu.make_async_copy(src, dst, rs).start()

    def sent_any(src, dst, ss, rs, dr, dc):
        @pl.when(jnp.logical_not(jnp.logical_and(dr == r, dc == c)))
        def _():
            rc(src, dst, ss, rs, dr, dc).wait_send()

    def arrived(dst, rs):
        pltpu.make_async_copy(dst, dst, rs).wait()

    def loop(n, body):
        lax.fori_loop(0, n, lambda k, _: (body(k), 0)[1], 0)

    def cols(k, n):
        return pl.ds(pl.multiple_of(k * n, n), n)

    loads = [
        pltpu.make_async_copy(a, b, w_sem.at[i])
        for i, (a, b) in enumerate(((wg_hbm, wg), (wu_hbm, wu), (wd_hbm, wd)))
    ]
    for load in loads:
        load.start()

    def tok_args(k):
        h, c2 = k // C, (k + c) % C
        return (
            tok.at[:, cols(h, Dr)], tokbuf.at[cols(r, PAD)], tok_s.at[k], tok_r.at[r], c * H + h, c2
        )

    def og_args(k):
        return (og, ogbuf.at[cols(r, PAD)], og_s.at[k], og_r.at[r], (r + k + 1) % R, c)

    loop(R, lambda k: start_any(*tok_args(k)))
    loop(R - 1, lambda k: rc(*og_args(k)).start())
    ogbuf[cols(r, PAD), :] = og[...]
    loop(R, lambda k: arrived(tokbuf.at[cols(k, PAD)], tok_r.at[k]))
    toks[...] = lax.dot_general(
        ex[...], tokbuf[...], rows_contract, preferred_element_type=f32
    ).astype(bf16)

    loads[0].wait()
    loads[1].wait()

    def x_args(k):
        return (xsend.at[k], xrecv.at[k], x_s.at[k], x_r.at[k], mate, c)

    def zp(k):
        return (z + k + 1) % Z

    def away(k):
        zz = zp(k)
        sub = zz * 2 + (1 - x)
        xsend[zz, :, 0:S] = mm(toks[...], wg[:, cols(sub, S)]).astype(bf16)
        xsend[zz, :, S : 2 * S] = mm(toks[...], wu[:, cols(sub, S)]).astype(bf16)
        rc(*x_args(zz)).start()

    loop(Z, away)

    def home(k):
        zz = zp(k)
        sub = zz * 2 + x
        own[zz, :, 0:S] = mm(toks[...], wg[:, cols(sub, S)])
        own[zz, :, S : 2 * S] = mm(toks[...], wu[:, cols(sub, S)])

    loop(Z, home)

    def z_args(k):
        return (zsend.at[zp(k)], zrecv.at[z], z_s.at[k], z_r.at[z], zp(k) * 2 + x, c)

    def along(k):
        zz = zp(k)
        arrived(xrecv.at[zz], x_r.at[zz])
        zsend[zz] = (own[zz] + xrecv[zz].astype(f32)).astype(bf16)
        rc(*z_args(k)).start()

    loop(Z - 1, along)

    def og_wait(k):
        src = (r + k + 1) % R
        arrived(ogbuf.at[cols(src, PAD)], og_r.at[src])

    loop(R - 1, og_wait)
    cot[...] = lax.dot_general(
        ex[...], ogbuf[...], rows_contract, preferred_element_type=f32
    ).astype(bf16)
    loads[2].wait()

    def gh_args(k):
        j = (c + k + 1) % C
        return (ghsend.at[j], ghrecv.at[c], gh_s.at[k], gh_r.at[c], r, j)

    def gh_step(k):
        j = (c + k + 1) % C
        ghsend[j] = mm_t(cot[...], wd[cols(j, S), :])
        rc(*gh_args(k)).start()

    loop(C - 1, gh_step)
    ghsum[...] = mm_t(cot[...], wd[cols(c, S), :])
    arrived(xrecv.at[z], x_r.at[z])
    gupd[...] = own[z] + xrecv[z].astype(f32)

    def gh_add(k):
        j = (c + k + 1) % C
        arrived(ghrecv.at[j], gh_r.at[j])
        ghsum[...] += ghrecv[j]

    loop(C - 1, gh_add)
    mine = r * C + c
    gh2 = (ghsum, ghfin, gh2_s.at[0], gh2_r.at[0], mine % R, mine // R)
    start_any(*gh2)

    def z_add(k):
        zz = zp(k)
        arrived(zrecv.at[zz], z_r.at[zz])
        gupd[...] += zrecv[zz].astype(f32)

    loop(Z - 1, z_add)
    held = c * R + r
    hsend[...] = (
        gupd[:, 0:S] * jax.nn.sigmoid(gupd[:, 0:S]) * gupd[:, S : 2 * S]
    ).astype(bf16)

    def h_args(k):
        return (
            hsend, hbuf.at[held % C], h_s.at[k], h_r.at[held % C], held // C, (c + k) % C
        )

    loop(C, lambda k: start_any(*h_args(k)))

    arrived(ghfin, gh2_r.at[0])
    gate, up, grad = gupd[:, 0:S], gupd[:, S : 2 * S], ghfin[...]
    sg = jax.nn.sigmoid(gate)
    tbuf[r, :, 0:S] = (grad * up * sg * (1.0 + gate * (1.0 - sg))).astype(bf16)
    tbuf[r, :, S : 2 * S] = (grad * (gate * sg)).astype(bf16)

    def t_args(k):
        return (tbuf.at[r], tbuf.at[r], t_s.at[k], t_r.at[r], zp(k) * 2 + x, c)

    def tf_args(k):
        slot = (z + k) % Z * 2 + x
        return (tbuf.at[slot], tbuf.at[slot], tf_s.at[k], t_r.at[slot], mate, c)

    loop(Z - 1, lambda k: rc(*t_args(k)).start())
    rc(*tf_args(0)).start()

    def h_use(k):
        arrived(hbuf.at[k], h_r.at[k])
        hid[:, cols(k, S)] = hbuf[k]
        hex_[:, cols(k, S)] = mm(ex[...], hbuf[k]).astype(bf16)

    loop(C, h_use)
    tile = S

    def po_step(k):
        po[:, cols(k, tile)] = mm(hex_[...], wd[:, cols(k, tile)])

    loop(po.shape[1] // tile, po_step)

    def fx_args(k):
        return (
            po.at[cols(k * 2 + 1 - x, PAD)], fxrecv.at[k], fx_s.at[k], fx_r.at[k], mate, c
        )

    loop(Z, lambda k: rc(*fx_args(zp(k))).start())

    acc[...] = jnp.zeros_like(acc)

    def use(slot):
        gg[:, cols(slot, S)] = tbuf[slot, :, 0:S]
        ug[:, cols(slot, S)] = tbuf[slot, :, S : 2 * S]
        wide = mm(ex[...], tbuf[slot]).astype(bf16)
        acc[...] += mm_t(wide[:, 0:S], wg[:, cols(slot, S)]) + mm_t(
            wide[:, S : 2 * S], wu[:, cols(slot, S)]
        )

    def near(k):
        slot = (z + k) % Z * 2 + x

        @pl.when(k > 0)
        def _():
            arrived(tbuf.at[slot], t_r.at[slot])
            rc(*tf_args(k)).start()

        use(slot)

    loop(Z, near)

    def fz_args(k):
        return (fzsend.at[zp(k)], fzrecv.at[z], fz_s.at[k], fz_r.at[z], zp(k) * 2 + x, c)

    def fz_step(k):
        zz = zp(k)
        arrived(fxrecv.at[zz], fx_r.at[zz])
        fzsend[zz] = po[cols(zz * 2 + x, PAD), :] + fxrecv[zz]
        rc(*fz_args(k)).start()

    loop(Z - 1, fz_step)

    def far(k):
        slot = (z + k) % Z * 2 + 1 - x
        arrived(tbuf.at[slot], t_r.at[slot])
        use(slot)

    loop(Z, far)

    def g_args(k):
        j = (c + k + 1) % C
        return (acc.at[cols(j, PAD * H)], grecv.at[c], g_s.at[k], g_r.at[c], r, j)

    loop(C - 1, lambda k: rc(*g_args(k)).start())

    arrived(fxrecv.at[z], fx_r.at[z])
    total = po[cols(r, PAD), :] + fxrecv[z]
    for k in range(Z - 1):
        arrived(fzrecv.at[zp(k)], fz_r.at[zp(k)])
        total = total + fzrecv[zp(k)]
    out[...] = total.astype(bf16)

    part = acc[cols(c, PAD * H), :]
    for k in range(C - 1):
        j = (c + k + 1) % C
        arrived(grecv.at[j], g_r.at[j])
        part = part + grecv[j]
    gsum[...] = part.astype(bf16)

    def g2_args(k):
        return (
            gsum.at[cols(k, PAD)], gtbuf.at[r % H], g2_s.at[k], g2_r.at[r % H], c * H + k, r // H
        )

    loop(H, lambda k: start_any(*g2_args(k)))
    for k in range(H):
        arrived(gtbuf.at[k], g2_r.at[k])
        gtok[:, k * Dr : (k + 1) * Dr] = gtbuf[k]

    loop(R, lambda k: sent_any(*tok_args(k)))
    loop(R - 1, lambda k: rc(*og_args(k)).wait_send())
    loop(Z, lambda k: rc(*x_args(k)).wait_send())
    loop(Z - 1, lambda k: rc(*z_args(k)).wait_send())
    loop(C - 1, lambda k: rc(*gh_args(k)).wait_send())
    sent_any(*gh2)
    loop(C, lambda k: sent_any(*h_args(k)))
    loop(Z - 1, lambda k: rc(*t_args(k)).wait_send())
    loop(Z, lambda k: rc(*tf_args(k)).wait_send())
    loop(Z, lambda k: rc(*fx_args(k)).wait_send())
    loop(Z - 1, lambda k: rc(*fz_args(k)).wait_send())
    loop(C - 1, lambda k: rc(*g_args(k)).wait_send())
    loop(H, lambda k: sent_any(*g2_args(k)))


def weight_grads(toks, gg, ug, hid, cot, dg, du, dd):
    dg[...] = lax.dot_general(
        toks[...], gg[...], rows_contract, preferred_element_type=f32
    ).astype(bf16)
    du[...] = lax.dot_general(
        toks[...], ug[...], rows_contract, preferred_element_type=f32
    ).astype(bf16)
    dd[...] = lax.dot_general(
        hid[...], cot[...], rows_contract, preferred_element_type=f32
    ).astype(bf16)


def per_device_kernels(R, C, tokens, w_gate, w_up, w_down, out_grad):
    tr, dc = tokens.shape
    T, Tp = tr * R, PAD * R
    dr, fc = w_gate.shape
    fr = w_down.shape[0]
    S = fc // R
    H, Z = R // C, R // 2
    expand = np.zeros((Tp, T), np.float32)
    for t in range(T):
        expand[t // tr * PAD + t % tr, t] = 1.0
    fill = ((0, PAD - tr), (0, 0))
    vm, anym = pl.BlockSpec(memory_space=pltpu.VMEM), pl.BlockSpec(memory_space=pl.ANY)
    shape = jax.ShapeDtypeStruct
    sem = lambda *n: pltpu.SemaphoreType.DMA(n)
    vmem = pltpu.VMEM
    out, gtok, toks, cot, hid, gg, ug = pl.pallas_call(
        functools.partial(layer, R, C),
        out_shape=(
            shape((PAD, dc), bf16), shape((PAD, dc), bf16), shape((T, dr), bf16),
            shape((T, dc), bf16), shape((T, fr), bf16), shape((T, fc), bf16), shape((T, fc), bf16),
        ),
        in_specs=[vm, vm, anym, anym, anym, vm],
        out_specs=(vm,) * 7,
        scratch_shapes=[
            vmem((dr, fc), bf16), vmem((dr, fc), bf16), vmem((fr, dc), bf16),
            vmem((Tp, dr), bf16), vmem((Tp, dc), bf16),
            vmem((Z, T, 2 * S), f32), vmem((Z, T, 2 * S), bf16), vmem((Z, T, 2 * S), bf16),
            vmem((Z, T, 2 * S), bf16), vmem((Z, T, 2 * S), bf16), vmem((T, 2 * S), f32),
            vmem((C, T, S), f32), vmem((C, T, S), f32), vmem((T, S), f32), vmem((T, S), f32),
            vmem((T, S), bf16), vmem((C, T, S), bf16), vmem((R, T, 2 * S), bf16), vmem((Tp, fr), bf16),
            vmem((Tp, dc), f32), vmem((Z, PAD, dc), f32), vmem((Z, PAD, dc), f32), vmem((Z, PAD, dc), f32),
            vmem((Tp, dr), f32), vmem((C, PAD * H, dr), f32), vmem((PAD * H, dr), bf16), vmem((H, PAD, dr), bf16),
            sem(3), sem(R), sem(R), sem(R), sem(R), sem(Z), sem(Z), sem(Z), sem(Z), sem(C), sem(C), sem(1), sem(1),
            sem(C), sem(C), sem(Z), sem(R), sem(Z), sem(Z), sem(Z), sem(Z), sem(Z), sem(C), sem(C), sem(H), sem(H),
        ],
        compiler_params=pltpu.CompilerParams(
            has_side_effects=True, vmem_limit_bytes=VMEM_LIMIT
        ),
    )(
        jnp.pad(tokens, fill), jnp.pad(out_grad, fill), w_gate, w_up, w_down,
        jnp.asarray(expand, bf16),
    )
    steps = 8
    whole = lambda a: pl.BlockSpec(a.shape, lambda i: (0, 0))
    part = lambda a: pl.BlockSpec((a.shape[0], a.shape[1] // steps), lambda i: (0, i))
    block = lambda n, m: pl.BlockSpec((n // steps, m), lambda i: (i, 0))
    dg, du, dd = pl.pallas_call(
        weight_grads,
        grid=(steps,),
        out_shape=(shape((dr, fc), bf16), shape((dr, fc), bf16), shape((fr, dc), bf16)),
        in_specs=[part(toks), whole(gg), whole(ug), part(hid), whole(cot)],
        out_specs=(block(dr, fc), block(dr, fc), block(fr, dc)),
        compiler_params=pltpu.CompilerParams(vmem_limit_bytes=VMEM_LIMIT),
    )(toks, gg, ug, hid, cot)
    return out[:tr], gtok[:tr], dg, du, dd


VMEM_LIMIT = 52 * 1024 * 1024


def solution(mesh):
    spec = P("row", "col")
    R, C = mesh.shape["row"], mesh.shape["col"]

    def run(tokens, w_gate, w_up, w_down, out_grad):
        lanes = w_gate.shape[1] // R
        aligned = lanes % 128 == 0 and w_gate.shape[0] % 1024 == 0 and tokens.shape[0] <= PAD
        if aligned and R == 2 * C:
            return per_device_kernels(R, C, tokens, w_gate, w_up, w_down, out_grad)
        return per_device(tokens, w_gate, w_up, w_down, out_grad)

    return jax.shard_map(
        run, mesh=mesh, in_specs=(spec,) * 5, out_specs=(spec,) * 5, check_vma=False
    )
```

```python
import functools

import jax
import jax.numpy as jnp
import numpy as np
from jax import lax
from jax.experimental import pallas as pl
from jax.experimental.pallas import tpu as pltpu
from jax.sharding import PartitionSpec as P

rows_contract = (((0,), (0,)), ((), ()))
cols_contract = (((1,), (1,)), ((), ()))


def broadcast(x, axis, root):
    mine = lax.axis_index(axis) == root
    return lax.psum(jnp.where(mine, x, jnp.zeros_like(x)), axis)


def per_device(tokens, w_gate, w_up, w_down, out_grad):
    row_index = lax.axis_index("row")
    col_index = lax.axis_index("col")
    tok_rows = tokens.shape[0]
    ff_cols = w_gate.shape[1]
    tokens_all, cotangent_all = (
        lax.all_gather(tokens, "row", axis=0, tiled=True),
        lax.all_gather(out_grad, "row", axis=0, tiled=True),
    )

    def to_row_blocks(matrix):
        piece_cols = matrix.shape[1] // 2
        picked = lax.dynamic_slice_in_dim(matrix, row_index % 2 * piece_cols, piece_cols, 1)
        return broadcast(picked, "col", row_index // 2)

    def to_col_blocks(matrix):
        pieces = []
        for offset in range(2):
            pieces.append(broadcast(matrix, "row", 2 * col_index + offset))
        return jnp.concatenate(pieces, axis=1)

    def col_total(matrix):
        return lax.psum(matrix, "col")

    tokens_rows = to_row_blocks(tokens_all)
    block = tokens_rows
    gate_up = lax.psum_scatter(
        jnp.concatenate(
            [
                jnp.dot(block, w_gate, preferred_element_type=jnp.float32),
                jnp.dot(block, w_up, preferred_element_type=jnp.float32),
            ],
            axis=1,
        ),
        "row",
        scatter_dimension=0,
        tiled=True,
    )
    gate = gate_up[:, :ff_cols]
    up = gate_up[:, ff_cols:]
    sigmoid_gate = jax.nn.sigmoid(gate)
    activated = gate * sigmoid_gate
    hidden_share = (activated * up).astype(jnp.bfloat16)
    hidden_all = lax.all_gather(hidden_share, "row", axis=0, tiled=True)
    hidden_rows = to_row_blocks(hidden_all)
    block = hidden_rows
    output = lax.psum_scatter(
        jnp.dot(block, w_down, preferred_element_type=jnp.float32),
        "row",
        scatter_dimension=0,
        tiled=True,
    ).astype(jnp.bfloat16)
    grad_down = lax.dot_general(
        hidden_rows, cotangent_all, rows_contract, preferred_element_type=jnp.float32
    ).astype(jnp.bfloat16)
    hidden_part = lax.dot_general(
        cotangent_all, w_down, cols_contract, preferred_element_type=jnp.float32
    )
    grad_hidden = to_col_blocks(col_total(hidden_part))
    grad_share = lax.dynamic_slice_in_dim(grad_hidden, row_index * tok_rows, tok_rows, 0)
    gate_term = (grad_share * up * sigmoid_gate * (1.0 + gate * (1.0 - sigmoid_gate))).astype(
        jnp.bfloat16
    )
    up_term = (grad_share * activated).astype(jnp.bfloat16)
    gate_grads, up_grads = (
        lax.all_gather(gate_term, "row", axis=0, tiled=True),
        lax.all_gather(up_term, "row", axis=0, tiled=True),
    )
    grad_gate = lax.dot_general(
        tokens_rows, gate_grads, rows_contract, preferred_element_type=jnp.float32
    ).astype(jnp.bfloat16)
    grad_up = lax.dot_general(
        tokens_rows, up_grads, rows_contract, preferred_element_type=jnp.float32
    ).astype(jnp.bfloat16)
    input_part = lax.dot_general(
        gate_grads, w_gate, cols_contract, preferred_element_type=jnp.float32
    ) + lax.dot_general(up_grads, w_up, cols_contract, preferred_element_type=jnp.float32)
    input_cols = to_col_blocks(col_total(input_part))
    grad_tokens = lax.dynamic_slice_in_dim(input_cols, row_index * tok_rows, tok_rows, 0).astype(
        jnp.bfloat16
    )
    return (output, grad_tokens, grad_gate, grad_up, grad_down)


MESH = pl.DeviceIdType.MESH
PAD = 16
f32, bf16 = jnp.float32, jnp.bfloat16


def mm(a, b):
    return jnp.dot(a, b, preferred_element_type=f32)


def mm_t(a, b):
    return lax.dot_general(a, b, cols_contract, preferred_element_type=f32)


def layer(
    R, C,
    tok, og, wg_hbm, wu_hbm, wd_hbm, ex,
    out, gtok, toks, cot, hid, gg, ug,
    wg, wu, wd, tokbuf, ogbuf, own, xsend, xrecv, zsend, zrecv, gupd,
    ghsend, ghrecv, ghsum, ghfin, hsend, hbuf, tbuf, hex_, po, fxsend, fxrecv, fzsend, fzrecv,
    acc, grecv, gsum, gtbuf,
    w_sem, tok_s, tok2_s, tok_r, og_s, og2_s, og_r, x_s, x_r, z_s, z_r, gh_s, gh_r, gh2_s, gh2_r,
    h_s, h_r, t_s, t_r, tf_s, fx_s, fx_r, fz_s, fz_r, g_s, g_r, g2_s, g2_r,
):
    r, c = lax.axis_index("row"), lax.axis_index("col")
    H, Z = R // C, R // 2
    z, x = r // 2, r % 2
    mate = z * 2 + (1 - x)
    S = wg.shape[1] // R
    Dr = wg.shape[0]

    def rc(src, dst, ss, rs, dr, dc):
        return pltpu.make_async_remote_copy(
            src_ref=src, dst_ref=dst, send_sem=ss, recv_sem=rs,
            device_id=(dr, dc), device_id_type=MESH,
        )

    def start_any(src, dst, ss, rs, dr, dc):
        here = jnp.logical_and(dr == r, dc == c)

        @pl.when(jnp.logical_not(here))
        def _():
            rc(src, dst, ss, rs, dr, dc).start()

        @pl.when(here)
        def _():
            pltpu.make_async_copy(src, dst, rs).start()

    def sent_any(src, dst, ss, rs, dr, dc):
        @pl.when(jnp.logical_not(jnp.logical_and(dr == r, dc == c)))
        def _():
            rc(src, dst, ss, rs, dr, dc).wait_send()

    def arrived(dst, rs):
        pltpu.make_async_copy(dst, dst, rs).wait()

    def loop(n, body):
        lax.fori_loop(0, n, lambda k, _: (body(k), 0)[1], 0)

    def cols(k, n):
        return pl.ds(pl.multiple_of(k * n, n), n)

    loads = [
        pltpu.make_async_copy(a, b, w_sem.at[i])
        for i, (a, b) in enumerate(((wg_hbm, wg), (wu_hbm, wu), (wd_hbm, wd)))
    ]
    loads[0].start()
    loads[1].start()
    barrier = pltpu.get_barrier_semaphore()

    def greet(k):
        other = (r * C + c + k + 1) % (R * C)
        pl.semaphore_signal(
            barrier, inc=1, device_id=(other // C, other % C), device_id_type=MESH
        )

    loop(R * C - 1, greet)
    pl.semaphore_wait(barrier, R * C - 1)

    def zp(k):
        return (z + k + 1) % Z

    def tok_args(h):
        return (
            tok.at[:, cols(h, Dr)], tokbuf.at[cols(r, PAD)], tok_s.at[h], tok_r.at[r],
            c * H + h, r % C,
        )

    def tok2_args(i):
        src = c + i // (C - 1) * C
        slot = tokbuf.at[cols(src, PAD)]
        return (slot, slot, tok2_s.at[i], tok_r.at[src], r, (c + i % (C - 1) + 1) % C)

    def og_args(k):
        return (og, ogbuf.at[cols(r, PAD)], og_s.at[k], og_r.at[r], zp(k) * 2 + x, c)

    def og2_args(k):
        src = (z + k) % Z * 2 + x
        slot = ogbuf.at[cols(src, PAD)]
        return (slot, slot, og2_s.at[k], og_r.at[src], mate, c)

    def og_own():
        return (og, ogbuf.at[cols(r, PAD)], og2_s.at[0], og_r.at[r], mate, c)

    loop(H, lambda h: start_any(*tok_args(h)))
    loop(Z - 1, lambda k: rc(*og_args(k)).start())
    rc(*og_own()).start()
    loads[2].start()
    ogbuf[cols(r, PAD), :] = og[...]

    def tok_pass(m):
        src = c + m * C
        arrived(tokbuf.at[cols(src, PAD)], tok_r.at[src])
        loop(C - 1, lambda k: rc(*tok2_args(m * (C - 1) + k)).start())

    loop(H, tok_pass)

    def tok_wait(k):
        @pl.when(k % C != c)
        def _():
            arrived(tokbuf.at[cols(k, PAD)], tok_r.at[k])

    loop(R, tok_wait)
    toks[...] = lax.dot_general(
        ex[...], tokbuf[...], rows_contract, preferred_element_type=f32
    ).astype(bf16)

    loads[0].wait()
    loads[1].wait()

    def x_args(k):
        return (xsend.at[k], xrecv.at[k], x_s.at[k], x_r.at[k], mate, c)

    def away(k):
        zz = zp(k)
        sub = zz * 2 + (1 - x)
        xsend[zz, :, 0:S] = mm(toks[...], wg[:, cols(sub, S)]).astype(bf16)
        xsend[zz, :, S : 2 * S] = mm(toks[...], wu[:, cols(sub, S)]).astype(bf16)
        rc(*x_args(zz)).start()

        @pl.when(k > 0)
        def _():
            src = (z + k) % Z * 2 + x
            arrived(ogbuf.at[cols(src, PAD)], og_r.at[src])
            rc(*og2_args(k)).start()

    loop(Z, away)

    def home(k):
        zz = zp(k)
        sub = zz * 2 + x
        own[zz, :, 0:S] = mm(toks[...], wg[:, cols(sub, S)])
        own[zz, :, S : 2 * S] = mm(toks[...], wu[:, cols(sub, S)])

    def z_args(k):
        return (zsend.at[zp(k)], zrecv.at[z], z_s.at[k], z_r.at[z], zp(k) * 2 + x, c)

    def along(k):
        zz = zp(k)
        arrived(xrecv.at[zz], x_r.at[zz])
        zsend[zz] = (own[zz] + xrecv[zz].astype(f32)).astype(bf16)
        rc(*z_args(k)).start()

    home(0)
    along(0)

    def og_wait(k):
        src = (z + k) % Z * 2 + 1 - x
        arrived(ogbuf.at[cols(src, PAD)], og_r.at[src])

    loop(Z, og_wait)
    cot[...] = lax.dot_general(
        ex[...], ogbuf[...], rows_contract, preferred_element_type=f32
    ).astype(bf16)
    loads[2].wait()

    def gh_args(k):
        j = (c + k + 1) % C
        return (ghsend.at[j], ghrecv.at[c], gh_s.at[k], gh_r.at[c], r, j)

    def gh_step(k):
        j = (c + k + 1) % C
        ghsend[j] = mm_t(cot[...], wd[cols(j, S), :])
        rc(*gh_args(k)).start()

    gh_step(0)

    def turn(k):
        home(k + 1)
        along(k + 1)
        gh_step(k + 1)

    loop(Z - 2, turn)
    home(Z - 1)
    ghsum[...] = mm_t(cot[...], wd[cols(c, S), :])
    arrived(xrecv.at[z], x_r.at[z])
    gupd[...] = own[z] + xrecv[z].astype(f32)

    def gh_add(k):
        j = (c + k + 1) % C
        arrived(ghrecv.at[j], gh_r.at[j])
        ghsum[...] += ghrecv[j]

    loop(C - 1, gh_add)
    mine = r * C + c
    gh2 = (ghsum, ghfin, gh2_s.at[0], gh2_r.at[0], mine % R, mine // R)
    start_any(*gh2)

    def z_add(k):
        zz = zp(k)
        arrived(zrecv.at[zz], z_r.at[zz])
        gupd[...] += zrecv[zz].astype(f32)

    loop(Z - 1, z_add)
    held = c * R + r
    hsend[...] = (
        gupd[:, 0:S] * jax.nn.sigmoid(gupd[:, 0:S]) * gupd[:, S : 2 * S]
    ).astype(bf16)

    h1 = (hsend, hbuf.at[held % C], h_s.at[0], h_r.at[held % C], held // C, held % C)
    start_any(*h1)

    def h_args(k):
        return (hbuf.at[c], hbuf.at[c], h_s.at[k], h_r.at[c], r, (c + k) % C)

    arrived(ghfin, gh2_r.at[0])
    gate, up, grad = gupd[:, 0:S], gupd[:, S : 2 * S], ghfin[...]
    sg = jax.nn.sigmoid(gate)
    tbuf[r, :, 0:S] = (grad * up * sg * (1.0 + gate * (1.0 - sg))).astype(bf16)
    tbuf[r, :, S : 2 * S] = (grad * (gate * sg)).astype(bf16)

    def t_args(k):
        return (tbuf.at[r], tbuf.at[r], t_s.at[k], t_r.at[r], zp(k) * 2 + x, c)

    def tf_args(k):
        slot = (z + k) % Z * 2 + x
        return (tbuf.at[slot], tbuf.at[slot], tf_s.at[k], t_r.at[slot], mate, c)

    loop(Z - 1, lambda k: rc(*t_args(k)).start())
    rc(*tf_args(0)).start()

    arrived(hbuf.at[c], h_r.at[c])
    loop(C - 1, lambda k: rc(*h_args(k + 1)).start())

    def h_use(k):
        j = (c + k) % C

        @pl.when(k > 0)
        def _():
            arrived(hbuf.at[j], h_r.at[j])

        hid[:, cols(j, S)] = hbuf[j]
        hex_[:, cols(j, S)] = mm(ex[...], hbuf[j]).astype(bf16)

    loop(C, h_use)
    tile = S

    def po_step(k):
        po[:, cols(k, tile)] = mm(hex_[...], wd[:, cols(k, tile)])

    loop(po.shape[1] // tile, po_step)

    def fx_cast(k):
        fxsend[k] = po[cols(k * 2 + 1 - x, PAD), :].astype(bf16)

    loop(Z, fx_cast)

    def fx_args(k):
        return (
            fxsend.at[k], fxrecv.at[k], fx_s.at[k], fx_r.at[k], mate, c
        )

    loop(Z, lambda k: rc(*fx_args(zp(k))).start())

    acc[...] = jnp.zeros_like(acc)

    def use(slot):
        gg[:, cols(slot, S)] = tbuf[slot, :, 0:S]
        ug[:, cols(slot, S)] = tbuf[slot, :, S : 2 * S]
        wide = mm(ex[...], tbuf[slot]).astype(bf16)
        acc[...] += mm_t(wide[:, 0:S], wg[:, cols(slot, S)]) + mm_t(
            wide[:, S : 2 * S], wu[:, cols(slot, S)]
        )

    def near(k):
        slot = (z + k) % Z * 2 + x

        @pl.when(k > 0)
        def _():
            arrived(tbuf.at[slot], t_r.at[slot])
            rc(*tf_args(k)).start()

        use(slot)

    loop(Z, near)

    def fz_args(k):
        return (fzsend.at[zp(k)], fzrecv.at[z], fz_s.at[k], fz_r.at[z], zp(k) * 2 + x, c)

    def fz_step(k):
        zz = zp(k)
        arrived(fxrecv.at[zz], fx_r.at[zz])
        fzsend[zz] = (po[cols(zz * 2 + x, PAD), :] + fxrecv[zz].astype(f32)).astype(bf16)
        rc(*fz_args(k)).start()

    loop(Z - 1, fz_step)

    def far(k):
        slot = (z + k) % Z * 2 + 1 - x
        arrived(tbuf.at[slot], t_r.at[slot])
        use(slot)

    loop(Z, far)

    def g_args(k):
        j = (c + k + 1) % C
        return (acc.at[cols(j, PAD * H)], grecv.at[c], g_s.at[k], g_r.at[c], r, j)

    loop(C - 1, lambda k: rc(*g_args(k)).start())

    arrived(fxrecv.at[z], fx_r.at[z])
    total = po[cols(r, PAD), :] + fxrecv[z].astype(f32)
    for k in range(Z - 1):
        arrived(fzrecv.at[zp(k)], fz_r.at[zp(k)])
        total = total + fzrecv[zp(k)].astype(f32)
    out[...] = total.astype(bf16)

    part = acc[cols(c, PAD * H), :]
    for k in range(C - 1):
        j = (c + k + 1) % C
        arrived(grecv.at[j], g_r.at[j])
        part = part + grecv[j]
    gsum[...] = part.astype(bf16)

    def g2_args(k):
        return (
            gsum.at[cols(k, PAD)], gtbuf.at[r % H], g2_s.at[k], g2_r.at[r % H], c * H + k, r // H
        )

    loop(H, lambda k: start_any(*g2_args(k)))
    for k in range(H):
        arrived(gtbuf.at[k], g2_r.at[k])
        gtok[:, k * Dr : (k + 1) * Dr] = gtbuf[k]

    loop(H, lambda h: sent_any(*tok_args(h)))
    loop(H * (C - 1), lambda i: rc(*tok2_args(i)).wait_send())
    loop(Z - 1, lambda k: rc(*og_args(k)).wait_send())
    rc(*og_own()).wait_send()
    loop(Z - 1, lambda k: rc(*og2_args(k + 1)).wait_send())
    loop(Z, lambda k: rc(*x_args(k)).wait_send())
    loop(Z - 1, lambda k: rc(*z_args(k)).wait_send())
    loop(C - 1, lambda k: rc(*gh_args(k)).wait_send())
    sent_any(*gh2)
    sent_any(*h1)
    loop(C - 1, lambda k: rc(*h_args(k + 1)).wait_send())
    loop(Z - 1, lambda k: rc(*t_args(k)).wait_send())
    loop(Z, lambda k: rc(*tf_args(k)).wait_send())
    loop(Z, lambda k: rc(*fx_args(k)).wait_send())
    loop(Z - 1, lambda k: rc(*fz_args(k)).wait_send())
    loop(C - 1, lambda k: rc(*g_args(k)).wait_send())
    loop(H, lambda k: sent_any(*g2_args(k)))


def weight_grads(toks, gg, ug, hid, cot, dg, du, dd):
    dg[...] = lax.dot_general(
        toks[...], gg[...], rows_contract, preferred_element_type=f32
    ).astype(bf16)
    du[...] = lax.dot_general(
        toks[...], ug[...], rows_contract, preferred_element_type=f32
    ).astype(bf16)
    dd[...] = lax.dot_general(
        hid[...], cot[...], rows_contract, preferred_element_type=f32
    ).astype(bf16)


def per_device_kernels(R, C, tokens, w_gate, w_up, w_down, out_grad):
    tr, dc = tokens.shape
    T, Tp = tr * R, PAD * R
    dr, fc = w_gate.shape
    fr = w_down.shape[0]
    S = fc // R
    H, Z = R // C, R // 2
    expand = np.zeros((Tp, T), np.float32)
    for t in range(T):
        expand[t // tr * PAD + t % tr, t] = 1.0
    fill = ((0, PAD - tr), (0, 0))
    vm, anym = pl.BlockSpec(memory_space=pltpu.VMEM), pl.BlockSpec(memory_space=pl.ANY)
    shape = jax.ShapeDtypeStruct
    sem = lambda *n: pltpu.SemaphoreType.DMA(n)
    vmem = pltpu.VMEM
    out, gtok, toks, cot, hid, gg, ug = pl.pallas_call(
        functools.partial(layer, R, C),
        out_shape=(
            shape((PAD, dc), bf16), shape((PAD, dc), bf16), shape((T, dr), bf16),
            shape((T, dc), bf16), shape((T, fr), bf16), shape((T, fc), bf16), shape((T, fc), bf16),
        ),
        in_specs=[vm, vm, anym, anym, anym, vm],
        out_specs=(vm,) * 7,
        scratch_shapes=[
            vmem((dr, fc), bf16), vmem((dr, fc), bf16), vmem((fr, dc), bf16),
            vmem((Tp, dr), bf16), vmem((Tp, dc), bf16),
            vmem((Z, T, 2 * S), f32), vmem((Z, T, 2 * S), bf16), vmem((Z, T, 2 * S), bf16),
            vmem((Z, T, 2 * S), bf16), vmem((Z, T, 2 * S), bf16), vmem((T, 2 * S), f32),
            vmem((C, T, S), f32), vmem((C, T, S), f32), vmem((T, S), f32), vmem((T, S), f32),
            vmem((T, S), bf16), vmem((C, T, S), bf16), vmem((R, T, 2 * S), bf16), vmem((Tp, fr), bf16),
            vmem((Tp, dc), f32), vmem((Z, PAD, dc), bf16), vmem((Z, PAD, dc), bf16),
            vmem((Z, PAD, dc), bf16), vmem((Z, PAD, dc), bf16),
            vmem((Tp, dr), f32), vmem((C, PAD * H, dr), f32), vmem((PAD * H, dr), bf16), vmem((H, PAD, dr), bf16),
            sem(3), sem(H), sem(H * (C - 1)), sem(R), sem(Z), sem(Z), sem(R), sem(Z), sem(Z), sem(Z), sem(Z), sem(C), sem(C), sem(1), sem(1),
            sem(C), sem(C), sem(Z), sem(R), sem(Z), sem(Z), sem(Z), sem(Z), sem(Z), sem(C), sem(C), sem(H), sem(H),
        ],
        compiler_params=pltpu.CompilerParams(
            collective_id=0, has_side_effects=True, vmem_limit_bytes=VMEM_LIMIT
        ),
    )(
        jnp.pad(tokens, fill), jnp.pad(out_grad, fill), w_gate, w_up, w_down,
        jnp.asarray(expand, bf16),
    )
    steps = 8
    whole = lambda a: pl.BlockSpec(a.shape, lambda i: (0, 0))
    part = lambda a: pl.BlockSpec((a.shape[0], a.shape[1] // steps), lambda i: (0, i))
    block = lambda n, m: pl.BlockSpec((n // steps, m), lambda i: (i, 0))
    dg, du, dd = pl.pallas_call(
        weight_grads,
        grid=(steps,),
        out_shape=(shape((dr, fc), bf16), shape((dr, fc), bf16), shape((fr, dc), bf16)),
        in_specs=[part(toks), whole(gg), whole(ug), part(hid), whole(cot)],
        out_specs=(block(dr, fc), block(dr, fc), block(fr, dc)),
        compiler_params=pltpu.CompilerParams(vmem_limit_bytes=VMEM_LIMIT),
    )(toks, gg, ug, hid, cot)
    return out[:tr], gtok[:tr], dg, du, dd


VMEM_LIMIT = 52 * 1024 * 1024


def solution(mesh):
    spec = P("row", "col")
    R, C = mesh.shape["row"], mesh.shape["col"]

    def run(tokens, w_gate, w_up, w_down, out_grad):
        lanes = w_gate.shape[1] // R
        aligned = lanes % 128 == 0 and w_gate.shape[0] % 1024 == 0 and tokens.shape[0] <= PAD
        if aligned and R == 2 * C:
            return per_device_kernels(R, C, tokens, w_gate, w_up, w_down, out_grad)
        return per_device(tokens, w_gate, w_up, w_down, out_grad)

    return jax.shard_map(
        run, mesh=mesh, in_specs=(spec,) * 5, out_specs=(spec,) * 5, check_vma=False
    )
```
